32 devices in a mesh: runs: 2 (over x), space: 16 (over z, y, core).
Axes of the slice: x: 2, y: 2, z: 4, core: 2. Of those that a mesh axis runs over, the one named last changes fastest.
Arguments:
- tangent: float32 [1024, 256, 128], P('runs', 'space'), parts along dimension 0, may hold values from -400 to 400
- courant_x: float32 [512, 128], P(('runs', 'space')), parts along dimension 0, may hold values from -0.4 to 0.4
- courant_y: float32 [512, 128], P(('runs', 'space')), parts along dimension 0, may hold values from -0.4 to 0.4
Outputs:
- basis: float32 [1024, 256, 128], P('runs', 'space'), parts along dimension 0
- growth: float32 [1024, 512], P('runs'), parts along dimension 0
- log_growth: float32 [1024], P('runs'), parts along dimension 0
- first_factor: float32 [1024, 512], P('runs'), parts along dimension 0
The draws below stay inside these ranges and needn't reach their ends.
There are 2 independent parts, one for each index of `runs`. The reference program is written for one: setup_inputs(seed, part) draws one part's arguments, and reference() takes and returns one part's arrays. A program takes and returns all parts, laid end to end along the dimension named above; each array names one. Nothing has to cross between parts.
All inputs are finite; a program needn't handle non-finite values.
Results may differ from the reference program's by a relative error of at most 0.0012.
Values sent between devices are 32-bit elements; how exact they have to be, the bound alone decides.
A program may use at most 128 MiB of HBM per device.

```python
import math
import jax
import jax.numpy as jnp
from jax import lax

K = 512
NY = 128
NX = 256


def draw_tangent(key, part):
    noise_key, vector_key, row_key, common_key = jax.random.split(key, 4)
    vector_scale = jnp.exp(jax.random.uniform(vector_key, (K, 1, 1), jnp.float32) * math.log(10.0))
    ramp = (jnp.arange(NX, dtype=jnp.float32) / NX * math.log(3.0)).reshape(1, NX, 1)
    row_scale = jnp.exp(jax.random.uniform(row_key, (1, NX, 1), jnp.float32) * math.log(10.0 / 3.0) + ramp)
    own_share = math.sqrt(K) / 1500.0
    common = jax.random.truncated_normal(common_key, -4.0, 4.0, (1, NX, NY), jnp.float32)
    own = jax.random.truncated_normal(noise_key, -4.0, 4.0, (K, NX, NY), jnp.float32)
    base = (common + own_share * own) / (1.0 + own_share)
    return base * vector_scale * row_scale


def shard_levels(own_key, extent, cuts, least, top_value):
    def one(dim, blocks):
        steps = jax.random.uniform(jax.random.fold_in(jax.random.fold_in(own_key, 6), dim), (blocks,), jnp.float32, least / len(cuts), top_value / len(cuts))
        return jnp.repeat(jnp.exp(steps), extent[dim] // blocks).reshape((-1,) + (1,) * (len(extent) - dim - 1))

    loudness = one(*cuts[0])
    for cut in cuts[1:]:
        loudness = loudness * one(*cut)
    return loudness


def setup_inputs(seed: int = 0, part: int = 0) -> dict:
    key_list = jax.random.split(jax.random.key(seed), 4)
    part_keys = jax.random.split(jax.random.fold_in(key_list[3], part), 4)
    tangent = draw_tangent(jax.random.fold_in(jax.random.fold_in(key_list[3], part), 71), part)
    courant_x = jnp.clip(jax.random.uniform(part_keys[1], (NX, NY), jnp.float32, -0.4, 0.4) * shard_levels(part_keys[1], (NX, NY), ((0, 16),), -0.4, 0.0), -0.4, 0.4)
    courant_y = jnp.clip(jax.random.uniform(part_keys[2], (NX, NY), jnp.float32, -0.4, 0.4) * shard_levels(part_keys[2], (NX, NY), ((0, 16),), -0.4, 0.0), -0.4, 0.4)
    return dict(tangent=tangent, courant_x=courant_x, courant_y=courant_y)


diffusion_number = 0.2

def update(center, east_side, west_side, courant_x, courant_y):
    north_side = jnp.roll(center, -1, 2)
    south_side = jnp.roll(center, 1, 2)
    spread = east_side + west_side + north_side + south_side - 4.0 * center
    return center + diffusion_number * spread - 0.5 * courant_x * (east_side - west_side) - 0.5 * courant_y * (north_side - south_side)

def advance(field, courant_x, courant_y):
    return update(field, jnp.roll(field, -1, 1), jnp.roll(field, 1, 1), courant_x, courant_y)

def factorize(gram, flattened):
    lower = jnp.linalg.cholesky(gram)
    identity = jnp.eye(gram.shape[0], dtype=jnp.float32)
    inverse = lax.linalg.triangular_solve(lower, identity, left_side=True, lower=True)
    return (lower, jnp.dot(inverse, flattened, precision=lax.Precision.HIGHEST))

def reference(tangent, courant_x, courant_y):
    advanced = advance(advance(tangent, courant_x, courant_y), courant_x, courant_y)
    flattened = advanced.reshape(K, NX * NY)
    cells = NX * NY
    first_gram = jnp.dot(flattened, flattened.T, precision=lax.Precision.HIGHEST) / cells
    first_lower, first_basis = factorize(first_gram, flattened)
    second_gram = jnp.dot(first_basis, first_basis.T, precision=lax.Precision.HIGHEST) / cells
    second_lower, final_basis = factorize(second_gram, first_basis)
    growth = jnp.dot(first_lower, second_lower, precision=lax.Precision.HIGHEST).T
    log_growth = jnp.log(jnp.diagonal(first_lower)) + jnp.log(jnp.diagonal(second_lower))
    return (final_basis.reshape(K, NX, NY), growth, log_growth, first_lower.T)
```

```python
import functools

import jax
import jax.numpy as jnp
from jax import lax
from jax.experimental import pallas as pl
from jax.experimental.pallas import tpu as pltpu
from jax.sharding import PartitionSpec as P

diffusion_number = 0.2
T = 128
MICRO = 16
HIGHEST = lax.Precision.HIGHEST
MESH = pl.DeviceIdType.MESH
VMEM_LIMIT = 48 * 1024 * 1024


def dot(a, b, dims):
    return lax.dot_general(a, b, (dims, ((), ())), precision=HIGHEST, preferred_element_type=jnp.float32)


NN = ((1,), (0,))
NT = ((1,), (1,))
TN = ((0,), (0,))


def pair_list(blocks):
    return [(i, j) for i in range(blocks) for j in range(i, blocks)]


def gram_rows(vectors, devices):
    blocks = vectors // T
    rows = blocks * (blocks + 1) // 2 * T
    chunk = -(-rows // (devices * 8)) * 8
    return chunk, chunk * devices


def gram_into(v_ref, packed_ref):
    vectors, width = v_ref.shape
    blocks = vectors // T
    packed_ref[...] = jnp.zeros_like(packed_ref)

    def step(s, _):
        cols = pl.ds(pl.multiple_of(s * 256, 256), 256)
        at = 0
        for i in range(blocks):
            left = v_ref[i * T:(i + 1) * T, cols]
            for j in range(i, blocks):
                packed_ref[at:at + T, :] += dot(left, v_ref[j * T:(j + 1) * T, cols], NT)
                at += T
        return 0

    lax.fori_loop(0, width // 256, step, 0)


def advance_kernel(w_ref, low_ref, high_ref, coef_ref, v_ref, packed_ref):
    vectors = v_ref.shape[0]
    nx = v_ref.shape[1] // T
    kc = 32

    def step(s, _):
        k0 = pl.multiple_of(s * kc, kc)

        def row(e):
            if e < 2:
                return low_ref[pl.ds(e * vectors + k0, kc), :]
            if e >= nx + 2:
                return high_ref[pl.ds((e - nx - 2) * vectors + k0, kc), :]
            return w_ref[pl.ds(k0 * nx + (e - 2), kc, stride=nx), :]

        def apply(west, center, east, e):
            ce, cw, cn, cs = [coef_ref[f, e - 1:e, :] for f in range(4)]
            north = pltpu.roll(center, T - 1, 1)
            south = pltpu.roll(center, 1, 1)
            return ((1.0 - 4.0 * diffusion_number) * center + (ce * east + cw * west)) + (cn * north + cs * south)

        zero = [row(0), row(1)]
        one = []
        for e in range(1, nx + 3):
            zero.append(row(e + 1))
            one.append(apply(zero[-3], zero[-2], zero[-1], e))
            if e >= 3:
                x = e - 3
                v_ref[pl.ds(k0, kc), x * T:(x + 1) * T] = apply(one[-3], one[-2], one[-1], e - 1)
        return 0

    lax.fori_loop(0, vectors // kc, step, 0)
    gram_into(v_ref, packed_ref)


def eliminate(block):
    m = MICRO
    lane = lax.broadcasted_iota(jnp.int32, (m, T), 1)
    sub = lax.broadcasted_iota(jnp.int32, (m, T), 0)
    rows128 = lax.broadcasted_iota(jnp.int32, (T, T), 0)
    lanes128 = lax.broadcasted_iota(jnp.int32, (T, T), 1)
    rest = jnp.concatenate([block, (rows128 == lanes128).astype(jnp.float32)], axis=1)
    uppers, inverses = [], []
    for p in range(T // m):
        panel = rest[:m]
        left = panel[:, :T]
        cols = [jnp.broadcast_to(left[:, p * m + j:p * m + j + 1], (m, T)) for j in range(m)]
        diag = jnp.ones((m, T), jnp.float32)
        for j in range(m):
            d = cols[j][j:j + 1, :]
            mult = jnp.where(sub > j, cols[j] * (1.0 / d), 0.0)
            diag = jnp.where(sub == j, d, diag)
            for k in range(j + 1, m):
                cols[k] = cols[k] - mult * cols[k][j:j + 1, :]
            wide = jnp.concatenate([mult, mult], axis=1)
            panel = panel - wide * panel[j:j + 1, :]
        scale = lax.rsqrt(diag)
        upper = jnp.where(lane >= sub + p * m, panel[:, :T] * scale, 0.0)
        inverse = panel[:, T:] * scale
        uppers.append(upper)
        inverses.append(inverse)
        if p + 1 < T // m:
            product = dot(upper, jnp.concatenate([upper, inverse], axis=1), TN)
            rest = rest[m:] - product[(p + 1) * m:]
    return jnp.concatenate(uppers, axis=0), jnp.concatenate(inverses, axis=0)


def factor_into(packed_ref, cells, z_ref, row_ref, upper_ref, inverse_ref):
    vectors = z_ref.shape[0]
    blocks = vectors // T
    z_ref[...] = jnp.zeros_like(z_ref)
    for at, (i, j) in enumerate(pair_list(blocks)):
        z_ref[i * T:(i + 1) * T, j * T:(j + 1) * T] = packed_ref[at * T:(at + 1) * T, :] / cells
    block_of = lax.broadcasted_iota(jnp.int32, (T, vectors), 1) // T

    def step(b, _):
        here = pl.ds(pl.multiple_of(b * T, T), T)
        upper, inverse = eliminate(z_ref[here, here])
        row_ref[...] = dot(inverse, z_ref[here, :], NN)
        row_ref[:, here] = inverse
        row = row_ref[...]
        upper_ref[here, :] = jnp.where(block_of > b, row, 0.0)
        upper_ref[here, here] = upper
        inverse_ref[here, :] = jnp.where(block_of <= b, row, 0.0)

        def below(c, _):
            there = pl.ds(pl.multiple_of(c * T, T), T)
            old = jnp.where(block_of == b, 0.0, z_ref[there, :])
            z_ref[there, :] = old - dot(row_ref[:, there], row_ref[...], TN)
            return 0

        lax.fori_loop(b + 1, blocks, below, 0)
        return 0

    lax.fori_loop(0, blocks, step, 0)


def first_kernel(cells, packed_ref, v_ref, upper_ref, q_ref, out_ref, z_ref, row_ref, inverse_ref):
    vectors, width = v_ref.shape
    factor_into(packed_ref, cells, z_ref, row_ref, upper_ref, inverse_ref)

    def step(s, _):
        cols = pl.ds(pl.multiple_of(s * 256, 256), 256)
        for i in range(vectors // T):
            q_ref[i * T:(i + 1) * T, cols] = dot(
                inverse_ref[i * T:(i + 1) * T, :(i + 1) * T], v_ref[:(i + 1) * T, cols], NN
            )
        return 0

    lax.fori_loop(0, width // 256, step, 0)
    gram_into(q_ref, out_ref)


def second_kernel(cells, packed_ref, q_ref, first_ref, basis_ref, growth_ref, log_ref, z_ref, row_ref, inverse_ref, upper_ref):
    vectors, width = q_ref.shape
    nx = width // T
    factor_into(packed_ref, cells, z_ref, row_ref, upper_ref, inverse_ref)

    def step(s, _):
        cols = pl.ds(pl.multiple_of(s * 256, 256), 256)
        for i in range(vectors // T):
            value = dot(inverse_ref[i * T:(i + 1) * T, :(i + 1) * T], q_ref[:(i + 1) * T, cols], NN)
            for h in range(2):
                basis_ref[pl.ds(i * T * nx + 2 * s + h, T, stride=nx), :] = value[:, h * T:(h + 1) * T]
        return 0

    lax.fori_loop(0, width // 256, step, 0)
    rows = lax.broadcasted_iota(jnp.int32, (T, T), 0)
    lanes = lax.broadcasted_iota(jnp.int32, (T, T), 1)
    for i in range(vectors // T):
        here = slice(i * T, (i + 1) * T)
        growth_ref[here, :] = dot(upper_ref[here, i * T:], first_ref[i * T:, :], NN)
        one = jnp.sum(jnp.where(rows == lanes, first_ref[here, here], 0.0), axis=0, keepdims=True)
        two = jnp.sum(jnp.where(rows == lanes, upper_ref[here, here], 0.0), axis=0, keepdims=True)
        log_ref[i:i + 1, :] = jnp.log(one) + jnp.log(two)


def reduce_kernel(n, x_ref, o_ref, pair_buf, sum_buf, recv_buf, pair_s, pair_r, rs_s, rs_r, ag_s, ag_r, fw_s, fw_r):
    chips = n // 2
    total = x_ref.shape[0]
    half = total // 2
    chunk = half // chips
    me = lax.axis_index("space")
    chip = me // 2
    core = me % 2
    partner = chip * 2 + (1 - core)

    def peer(k):
        return lax.rem(chip + k, chips) * 2 + core

    def source(k):
        return lax.rem(chip + chips - k, chips)

    barrier = pltpu.get_barrier_semaphore()
    pl.semaphore_signal(barrier, inc=1, device_id={"space": partner}, device_id_type=MESH)

    def greet(k, _):
        pl.semaphore_signal(barrier, inc=1, device_id={"space": peer(k)}, device_id_type=MESH)
        return 0

    lax.fori_loop(1, chips, greet, 0)
    pl.semaphore_wait(barrier, chips)

    mine = pl.multiple_of(core * half, 8)
    other = pl.multiple_of((1 - core) * half, 8)
    swap = pltpu.make_async_remote_copy(
        src_ref=x_ref.at[pl.ds(other, half)], dst_ref=pair_buf, send_sem=pair_s, recv_sem=pair_r,
        device_id={"space": partner}, device_id_type=MESH)
    swap.start()
    swap.wait()
    sum_buf[...] = x_ref[pl.ds(mine, half), :] + pair_buf[...]

    def scatter(k):
        to = lax.rem(chip + k, chips)
        return pltpu.make_async_remote_copy(
            src_ref=sum_buf.at[pl.ds(pl.multiple_of(to * chunk, 8), chunk)], dst_ref=recv_buf.at[k],
            send_sem=rs_s.at[k], recv_sem=rs_r.at[k], device_id={"space": peer(k)}, device_id_type=MESH)

    def start_scatter(k, _):
        scatter(k).start()
        return 0

    lax.fori_loop(1, chips, start_scatter, 0)
    own = pl.ds(pl.multiple_of(chip * chunk, 8), chunk)
    own_out = pl.ds(pl.multiple_of(mine + chip * chunk, 8), chunk)

    def add(k, acc):
        scatter(k).wait_recv()
        return acc + recv_buf[k]

    o_ref[own_out, :] = lax.fori_loop(1, chips, add, sum_buf[own, :])

    def gather(k):
        return pltpu.make_async_remote_copy(
            src_ref=o_ref.at[own_out], dst_ref=o_ref.at[own_out],
            send_sem=ag_s.at[k], recv_sem=ag_r.at[k], device_id={"space": peer(k)}, device_id_type=MESH)

    def forward(k):
        at = pl.ds(pl.multiple_of(mine + source(k) * chunk, 8), chunk)
        return pltpu.make_async_remote_copy(
            src_ref=o_ref.at[at], dst_ref=o_ref.at[at],
            send_sem=fw_s.at[k], recv_sem=fw_r.at[k], device_id={"space": partner}, device_id_type=MESH)

    def start_gather(k, _):
        gather(k).start()
        return 0

    lax.fori_loop(1, chips, start_gather, 0)
    forward(0).start()

    def pass_on(k, _):
        gather(k).wait_recv()
        forward(k).start()
        return 0

    lax.fori_loop(1, chips, pass_on, 0)

    def finish(k, _):
        forward(k).wait()
        return 0

    lax.fori_loop(0, chips, finish, 0)

    def drain(k, _):
        scatter(k).wait_send()
        gather(k).wait_send()
        return 0

    lax.fori_loop(1, chips, drain, 0)


def whole(memory=pltpu.VMEM):
    return pl.BlockSpec(memory_space=memory)


def plain(kernel, outs, ins, scratch=()):
    return pl.pallas_call(
        kernel,
        out_shape=tuple(jax.ShapeDtypeStruct(s, jnp.float32) for s in outs),
        in_specs=[whole()] * ins,
        out_specs=tuple(whole() for _ in outs),
        scratch_shapes=[pltpu.VMEM(s, jnp.float32) for s in scratch],
        compiler_params=pltpu.CompilerParams(vmem_limit_bytes=VMEM_LIMIT),
    )


def all_reduce(packed, n):
    total = packed.shape[0]
    chips = n // 2
    half = total // 2
    sems = pltpu.SemaphoreType.DMA
    return pl.pallas_call(
        functools.partial(reduce_kernel, n),
        out_shape=jax.ShapeDtypeStruct(packed.shape, jnp.float32),
        in_specs=[whole()],
        out_specs=whole(),
        scratch_shapes=[
            pltpu.VMEM((half, T), jnp.float32),
            pltpu.VMEM((half, T), jnp.float32),
            pltpu.VMEM((chips, half // chips, T), jnp.float32),
            sems, sems,
            sems((chips,)), sems((chips,)), sems((chips,)), sems((chips,)), sems((chips,)), sems((chips,)),
        ],
        compiler_params=pltpu.CompilerParams(collective_id=0, has_side_effects=True, vmem_limit_bytes=VMEM_LIMIT),
    )(packed)


def body(tangent, courant_x, courant_y):
    vectors, nx, ny = tangent.shape
    n = lax.axis_size("space")
    width = nx * ny
    cells = float(width * n)

    def edge(a, b):
        rows = jnp.transpose(tangent[:, a:a + 2], (1, 0, 2)).reshape(2 * vectors, ny)
        return jnp.concatenate([rows, courant_x[b:b + 1], courant_y[b:b + 1], jnp.zeros((6, ny), jnp.float32)], axis=0)

    low = lax.ppermute(edge(nx - 2, nx - 1), "space", [(i, (i + 1) % n) for i in range(n)])
    high = lax.ppermute(edge(0, 0), "space", [((i + 1) % n, i) for i in range(n)])
    e = 2 * vectors
    cx = 0.5 * jnp.concatenate([low[e:e + 1], courant_x, high[e:e + 1]], axis=0)
    cy = 0.5 * jnp.concatenate([low[e + 1:e + 2], courant_y, high[e + 1:e + 2]], axis=0)
    coef = jnp.stack([diffusion_number - cx, diffusion_number + cx, diffusion_number - cy, diffusion_number + cy])
    total = gram_rows(vectors, n)[1]
    v, packed = plain(advance_kernel, [(vectors, width), (total, T)], 4)(
        tangent.reshape(vectors * nx, ny), low, high, coef)
    packed = all_reduce(packed, n)
    square = (vectors, vectors)
    row = (T, vectors)
    first_upper, q, packed = plain(
        functools.partial(first_kernel, cells), [square, (vectors, width), (total, T)], 2, [square, row, square],
    )(packed, v)
    packed = all_reduce(packed, n)
    basis, growth, log_growth = plain(
        functools.partial(second_kernel, cells), [(vectors * nx, ny), square, (vectors // T, T)], 3,
        [square, row, square, square],
    )(packed, q, first_upper)
    return basis.reshape(tangent.shape), growth, log_growth.reshape(vectors), first_upper


def solution(mesh):
    return jax.shard_map(
        body,
        mesh=mesh,
        in_specs=(P("runs", "space", None), P(("runs", "space"), None), P(("runs", "space"), None)),
        out_specs=(P("runs", "space", None), P("runs", None), P("runs"), P("runs", None)),
        check_vma=False,
    )
```

```python
import functools

import jax
import jax.numpy as jnp
from jax import lax
from jax.experimental import pallas as pl
from jax.experimental.pallas import tpu as pltpu
from jax.sharding import PartitionSpec as P

diffusion_number = 0.2
T = 128
B = 256
MICRO = 16
HIGHEST = lax.Precision.HIGHEST
MESH = pl.DeviceIdType.MESH
VMEM_LIMIT = 48 * 1024 * 1024


def dot(a, b, dims):
    return lax.dot_general(a, b, (dims, ((), ())), precision=HIGHEST, preferred_element_type=jnp.float32)


NN = ((1,), (0,))
NT = ((1,), (1,))
TN = ((0,), (0,))


def pair_list(blocks):
    return [(i, j) for i in range(blocks) for j in range(i, blocks)]


def gram_rows(vectors, devices):
    blocks = vectors // T
    rows = blocks * (blocks + 1) // 2 * T
    chunk = -(-rows // (devices * 8)) * 8
    return chunk, chunk * devices


def split(value):
    high = value.astype(jnp.bfloat16)
    rest = value - high.astype(jnp.float32)
    middle = rest.astype(jnp.bfloat16)
    low = (rest - middle.astype(jnp.float32)).astype(jnp.bfloat16)
    return high, middle, low


def parts_left(high, middle, low, axis):
    return jnp.concatenate([low, high, middle, middle, high, high], axis=axis)


def parts_right(high, middle, low, axis):
    return jnp.concatenate([high, low, middle, high, middle, high], axis=axis)


def product(a, b, dims):
    return lax.dot_general(a, b, (dims, ((), ())), preferred_element_type=jnp.float32)


def gram_into(v_refs, acc_ref):
    vectors = v_refs[0].shape[0]
    wide = vectors // B
    acc_ref[...] = jnp.zeros_like(acc_ref)
    for v_ref in v_refs:

        def step(s, _):
            cols = pl.ds(pl.multiple_of(s * B, B), B)
            parts = [split(v_ref[i * B:(i + 1) * B, cols]) for i in range(wide)]
            at = 0
            for i in range(wide):
                high, middle, low = parts[i]
                same = jnp.concatenate([middle, high], axis=1)
                acc_ref[at] += product(same, same, NT)
                mixed = jnp.concatenate([low, middle], axis=1)
                acc_ref[at + 1] += product(jnp.concatenate([high, high], axis=1), mixed, NT)
                at += 2
            for i in range(wide):
                for j in range(i + 1, wide):
                    acc_ref[at] += product(parts_left(*parts[i], 1), parts_right(*parts[j], 1), NT)
                    at += 1
            return 0

        lax.fori_loop(0, v_ref.shape[1] // B, step, 0)


def gram_scratch(vectors):
    wide = vectors // B
    return (2 * wide + wide * (wide - 1) // 2, B, B)


def pack(acc_ref, packed_ref, vectors, add_ref=None):
    wide = vectors // B
    blocks = {}
    for i in range(wide):
        mixed = acc_ref[2 * i + 1]
        blocks[i, i] = acc_ref[2 * i] + (mixed + mixed.T)
    at = 2 * wide
    for i in range(wide):
        for j in range(i + 1, wide):
            blocks[i, j] = acc_ref[at]
            at += 1
    r = B // T
    end = 0
    for i, j in pair_list(vectors // T):
        value = blocks[i // r, j // r][i % r * T:(i % r + 1) * T, j % r * T:(j % r + 1) * T]
        if add_ref is not None:
            value = value + add_ref[end:end + T, :]
        packed_ref[end:end + T, :] = value
        end += T
    if end < packed_ref.shape[0]:
        packed_ref[end:, :] = jnp.zeros((packed_ref.shape[0] - end, T), jnp.float32)


def lower_times(inverse_ref, split_refs, v_ref, emit):
    vectors, width = v_ref.shape
    wide = vectors // B

    def step(s, _):
        cols = pl.ds(pl.multiple_of(s * B, B), B)
        parts = [parts_right(*split(v_ref[k * B:(k + 1) * B, cols]), 0) for k in range(wide)]
        for i in range(wide):
            total = None
            for k in range(i + 1):
                left = parts_left(*[ref[i * B:(i + 1) * B, k * B:(k + 1) * B] for ref in split_refs], 1)
                term = product(left, parts[k], NN)
                total = term if total is None else total + term
            emit(i, s, cols, total)
        return 0

    lax.fori_loop(0, width // B, step, 0)


def split_into(inverse_ref, split_refs):
    for i in range(inverse_ref.shape[0] // T):
        here = slice(i * T, (i + 1) * T)
        for ref, value in zip(split_refs, split(inverse_ref[here, :])):
            ref[here, :] = value


def apply(west, center, east, coef_ref, e):
    ce, cw, cn, cs = [coef_ref[f, e:e + 1, :] for f in range(4)]
    north = pltpu.roll(center, T - 1, 1)
    south = pltpu.roll(center, 1, 1)
    return ((1.0 - 4.0 * diffusion_number) * center + (ce * east + cw * west)) + (cn * north + cs * south)


def two_steps(row, first, count, coef_ref, coef_at, store):
    zero = [row(first - 2), row(first - 1)]
    one = []
    for x in range(first - 1, first + count + 1):
        zero.append(row(x + 1))
        one.append(apply(*zero[-3:], coef_ref, coef_at(x)))
        if len(one) >= 3:
            store(x - 1, apply(*one[-3:], coef_ref, coef_at(x - 1)))


def interior_kernel(w_ref, coef_ref, v_ref, packed_ref, acc_ref):
    vectors = v_ref.shape[0]
    nx = v_ref.shape[1] // T + 4
    kc = 32

    def step(s, _):
        k0 = pl.multiple_of(s * kc, kc)

        def row(x):
            return w_ref[pl.ds(k0 * nx + x, kc, stride=nx), :]

        def store(x, value):
            v_ref[pl.ds(k0, kc), (x - 2) * T:(x - 1) * T] = value

        two_steps(row, 2, nx - 4, coef_ref, lambda x: x, store)
        return 0

    lax.fori_loop(0, vectors // kc, step, 0)
    gram_into([v_ref], acc_ref)
    pack(acc_ref, packed_ref, vectors)


def edge_kernel(nx, mine_ref, low_ref, high_ref, coef_ref, add_ref, v_ref, packed_ref, acc_ref):
    vectors = v_ref.shape[0]
    kc = 32

    def step(s, _):
        k0 = pl.multiple_of(s * kc, kc)

        def row(x):
            if x < 0:
                return low_ref[pl.ds((x + 2) * vectors + k0, kc), :]
            if x >= nx:
                return high_ref[pl.ds((x - nx) * vectors + k0, kc), :]
            at = x if x < 4 else x - nx + 8
            return mine_ref[pl.ds(at * vectors + k0, kc), :]

        def store(x, value):
            at = x if x < 2 else x - nx + 4
            v_ref[pl.ds(k0, kc), at * T:(at + 1) * T] = value

        two_steps(row, 0, 2, coef_ref, lambda x: x + 1, store)
        two_steps(row, nx - 2, 2, coef_ref, lambda x: x + 1, store)
        return 0

    lax.fori_loop(0, vectors // kc, step, 0)
    gram_into([v_ref], acc_ref)
    pack(acc_ref, packed_ref, vectors, add_ref)


def eliminate(block):
    m = MICRO
    lane = lax.broadcasted_iota(jnp.int32, (m, T), 1)
    sub = lax.broadcasted_iota(jnp.int32, (m, T), 0)
    rows128 = lax.broadcasted_iota(jnp.int32, (T, T), 0)
    lanes128 = lax.broadcasted_iota(jnp.int32, (T, T), 1)
    rest = jnp.concatenate([block, (rows128 == lanes128).astype(jnp.float32)], axis=1)
    uppers, inverses = [], []
    for p in range(T // m):
        panel = rest[:m]
        left = panel[:, :T]
        cols = [jnp.broadcast_to(left[:, p * m + j:p * m + j + 1], (m, T)) for j in range(m)]
        diag = jnp.ones((m, T), jnp.float32)
        for j in range(m):
            d = cols[j][j:j + 1, :]
            mult = jnp.where(sub > j, cols[j] * (1.0 / d), 0.0)
            diag = jnp.where(sub == j, d, diag)
            for k in range(j + 1, m):
                cols[k] = cols[k] - mult * cols[k][j:j + 1, :]
            wide = jnp.concatenate([mult, mult], axis=1)
            panel = panel - wide * panel[j:j + 1, :]
        scale = lax.rsqrt(diag)
        upper = jnp.where(lane >= sub + p * m, panel[:, :T] * scale, 0.0)
        inverse = panel[:, T:] * scale
        uppers.append(upper)
        inverses.append(inverse)
        if p + 1 < T // m:
            product = dot(upper, jnp.concatenate([upper, inverse], axis=1), TN)
            rest = rest[m:] - product[(p + 1) * m:]
    return jnp.concatenate(uppers, axis=0), jnp.concatenate(inverses, axis=0)


def factor_into(packed_ref, cells, z_ref, row_ref, upper_ref, inverse_ref):
    vectors = z_ref.shape[0]
    blocks = vectors // T
    z_ref[...] = jnp.zeros_like(z_ref)
    for at, (i, j) in enumerate(pair_list(blocks)):
        z_ref[i * T:(i + 1) * T, j * T:(j + 1) * T] = packed_ref[at * T:(at + 1) * T, :] / cells
    block_of = lax.broadcasted_iota(jnp.int32, (T, vectors), 1) // T

    def step(b, _):
        here = pl.ds(pl.multiple_of(b * T, T), T)
        upper, inverse = eliminate(z_ref[here, here])
        row_ref[...] = dot(inverse, z_ref[here, :], NN)
        row_ref[:, here] = inverse
        row = row_ref[...]
        upper_ref[here, :] = jnp.where(block_of > b, row, 0.0)
        upper_ref[here, here] = upper
        inverse_ref[here, :] = jnp.where(block_of <= b, row, 0.0)

        def below(c, _):
            there = pl.ds(pl.multiple_of(c * T, T), T)
            old = jnp.where(block_of == b, 0.0, z_ref[there, :])
            z_ref[there, :] = old - dot(row_ref[:, there], row_ref[...], TN)
            return 0

        lax.fori_loop(b + 1, blocks, below, 0)
        return 0

    lax.fori_loop(0, blocks, step, 0)


def first_kernel(cells, packed_ref, inner_ref, outer_ref, upper_ref, q_inner_ref, q_outer_ref, out_ref, z_ref, row_ref, inverse_ref, acc_ref, *split_refs):
    vectors = inner_ref.shape[0]
    factor_into(packed_ref, cells, z_ref, row_ref, upper_ref, inverse_ref)
    split_into(inverse_ref, split_refs)
    for v_ref, q_ref in ((inner_ref, q_inner_ref), (outer_ref, q_outer_ref)):

        def emit(i, s, cols, value):
            q_ref[i * B:(i + 1) * B, cols] = value

        lower_times(inverse_ref, split_refs, v_ref, emit)
    gram_into([q_inner_ref, q_outer_ref], acc_ref)
    pack(acc_ref, out_ref, vectors)


def second_kernel(cells, packed_ref, inner_ref, outer_ref, first_ref, basis_ref, growth_ref, log_ref, z_ref, row_ref, inverse_ref, upper_ref, *split_refs):
    vectors = inner_ref.shape[0]
    nx = basis_ref.shape[0] // vectors
    factor_into(packed_ref, cells, z_ref, row_ref, upper_ref, inverse_ref)
    split_into(inverse_ref, split_refs)

    def emit_inner(i, s, cols, value):
        for h in range(2):
            basis_ref[pl.ds(i * B * nx + 2 + 2 * s + h, B, stride=nx), :] = value[:, h * T:(h + 1) * T]

    def emit_outer(i, s, cols, value):
        for h in range(2):
            basis_ref[pl.ds(i * B * nx + s * (nx - 2) + h, B, stride=nx), :] = value[:, h * T:(h + 1) * T]

    lower_times(inverse_ref, split_refs, inner_ref, emit_inner)
    lower_times(inverse_ref, split_refs, outer_ref, emit_outer)
    rows = lax.broadcasted_iota(jnp.int32, (T, T), 0)
    lanes = lax.broadcasted_iota(jnp.int32, (T, T), 1)
    for i in range(vectors // T):
        here = slice(i * T, (i + 1) * T)
        growth_ref[here, :] = dot(upper_ref[here, i * T:], first_ref[i * T:, :], NN)
        one = jnp.sum(jnp.where(rows == lanes, first_ref[here, here], 0.0), axis=0, keepdims=True)
        two = jnp.sum(jnp.where(rows == lanes, upper_ref[here, here], 0.0), axis=0, keepdims=True)
        log_ref[i:i + 1, :] = jnp.log(one) + jnp.log(two)


def reduce_kernel(n, x_ref, o_ref, pair_buf, sum_buf, recv_buf, pair_s, pair_r, rs_s, rs_r, ag_s, ag_r, fw_s, fw_r):
    chips = n // 2
    total = x_ref.shape[0]
    half = total // 2
    chunk = half // chips
    me = lax.axis_index("space")
    chip = me // 2
    core = me % 2
    partner = chip * 2 + (1 - core)

    def peer(k):
        return lax.rem(chip + k, chips) * 2 + core

    def source(k):
        return lax.rem(chip + chips - k, chips)

    barrier = pltpu.get_barrier_semaphore()
    pl.semaphore_signal(barrier, inc=1, device_id={"space": partner}, device_id_type=MESH)

    def greet(k, _):
        pl.semaphore_signal(barrier, inc=1, device_id={"space": peer(k)}, device_id_type=MESH)
        return 0

    lax.fori_loop(1, chips, greet, 0)
    pl.semaphore_wait(barrier, chips)

    mine = pl.multiple_of(core * half, 8)
    other = pl.multiple_of((1 - core) * half, 8)

    def swap(k):
        at = lax.rem(chip + k, chips) * chunk
        return pltpu.make_async_remote_copy(
            src_ref=x_ref.at[pl.ds(pl.multiple_of(other + at, 8), chunk)],
            dst_ref=pair_buf.at[pl.ds(pl.multiple_of(at, 8), chunk)],
            send_sem=pair_s.at[k], recv_sem=pair_r.at[k],
            device_id={"space": partner}, device_id_type=MESH)

    def scatter(k):
        to = lax.rem(chip + k, chips)
        return pltpu.make_async_remote_copy(
            src_ref=sum_buf.at[pl.ds(pl.multiple_of(to * chunk, 8), chunk)], dst_ref=recv_buf.at[k],
            send_sem=rs_s.at[k], recv_sem=rs_r.at[k], device_id={"space": peer(k)}, device_id_type=MESH)

    def start_swap(k, _):
        swap(lax.rem(k, chips)).start()
        return 0

    lax.fori_loop(1, chips + 1, start_swap, 0)

    def start_scatter(i, _):
        k = lax.rem(i, chips)
        swap(k).wait_recv()
        at = lax.rem(chip + k, chips) * chunk
        here = pl.ds(pl.multiple_of(at, 8), chunk)
        sum_buf[here, :] = x_ref[pl.ds(pl.multiple_of(mine + at, 8), chunk), :] + pair_buf[here, :]
        return 0

    def send_on(k, _):
        start_scatter(k, 0)
        scatter(k).start()
        return 0

    lax.fori_loop(1, chips, send_on, 0)
    start_scatter(0, 0)
    own = pl.ds(pl.multiple_of(chip * chunk, 8), chunk)
    own_out = pl.ds(pl.multiple_of(mine + chip * chunk, 8), chunk)

    def add(k, acc):
        scatter(k).wait_recv()
        return acc + recv_buf[k]

    o_ref[own_out, :] = lax.fori_loop(1, chips, add, sum_buf[own, :])

    def gather(k):
        return pltpu.make_async_remote_copy(
            src_ref=o_ref.at[own_out], dst_ref=o_ref.at[own_out],
            send_sem=ag_s.at[k], recv_sem=ag_r.at[k], device_id={"space": peer(k)}, device_id_type=MESH)

    def forward(k):
        at = pl.ds(pl.multiple_of(mine + source(k) * chunk, 8), chunk)
        return pltpu.make_async_remote_copy(
            src_ref=o_ref.at[at], dst_ref=o_ref.at[at],
            send_sem=fw_s.at[k], recv_sem=fw_r.at[k], device_id={"space": partner}, device_id_type=MESH)

    def start_gather(k, _):
        gather(k).start()
        return 0

    lax.fori_loop(1, chips, start_gather, 0)
    forward(0).start()

    def pass_on(k, _):
        gather(k).wait_recv()
        forward(k).start()
        return 0

    lax.fori_loop(1, chips, pass_on, 0)

    def finish(k, _):
        forward(k).wait()
        return 0

    lax.fori_loop(0, chips, finish, 0)

    def drain_swap(k, _):
        swap(k).wait_send()
        return 0

    lax.fori_loop(0, chips, drain_swap, 0)

    def drain(k, _):
        scatter(k).wait_send()
        gather(k).wait_send()
        return 0

    lax.fori_loop(1, chips, drain, 0)


def whole(memory=pltpu.VMEM):
    return pl.BlockSpec(memory_space=memory)


def plain(kernel, outs, ins, scratch=(), splits=0, cost=None):
    scratch_shapes = [pltpu.VMEM(shape, jnp.float32) for shape in scratch]
    if splits:
        scratch_shapes += [pltpu.VMEM((splits, splits), jnp.bfloat16)] * 3
    return pl.pallas_call(
        kernel,
        out_shape=tuple(jax.ShapeDtypeStruct(shape, jnp.float32) for shape in outs),
        in_specs=[whole()] * ins,
        out_specs=tuple(whole() for _ in outs),
        scratch_shapes=scratch_shapes,
        compiler_params=pltpu.CompilerParams(vmem_limit_bytes=VMEM_LIMIT),
        cost_estimate=cost,
    )


def all_reduce(packed, n):
    total = packed.shape[0]
    chips = n // 2
    half = total // 2
    sems = pltpu.SemaphoreType.DMA
    return pl.pallas_call(
        functools.partial(reduce_kernel, n),
        out_shape=jax.ShapeDtypeStruct(packed.shape, jnp.float32),
        in_specs=[whole()],
        out_specs=whole(),
        scratch_shapes=[
            pltpu.VMEM((half, T), jnp.float32),
            pltpu.VMEM((half, T), jnp.float32),
            pltpu.VMEM((chips, half // chips, T), jnp.float32),
            sems((chips,)), sems((chips,)),
            sems((chips,)), sems((chips,)), sems((chips,)), sems((chips,)), sems((chips,)), sems((chips,)),
        ],
        compiler_params=pltpu.CompilerParams(collective_id=0, has_side_effects=True, vmem_limit_bytes=VMEM_LIMIT),
    )(packed)


def body(tangent, courant_x, courant_y):
    vectors, nx, ny = tangent.shape
    n = lax.axis_size("space")
    width = nx * ny
    cells = float(width * n)

    pick = jnp.concatenate([tangent[:, :4], tangent[:, nx - 4:]], axis=1)
    mine = jnp.transpose(pick, (1, 0, 2)).reshape(8 * vectors, ny)

    def edge(a, b):
        rows = mine[a * vectors:(a + 2) * vectors]
        return jnp.concatenate([rows, courant_x[b:b + 1], courant_y[b:b + 1], jnp.zeros((6, ny), jnp.float32)], axis=0)

    def coefficients(x, y):
        x, y = 0.5 * x, 0.5 * y
        return jnp.stack([diffusion_number - x, diffusion_number + x, diffusion_number - y, diffusion_number + y])

    low = lax.ppermute(edge(6, nx - 1), "space", [(i, (i + 1) % n) for i in range(n)])
    high = lax.ppermute(edge(0, 0), "space", [((i + 1) % n, i) for i in range(n)])
    e = 2 * vectors
    cx = jnp.concatenate([low[e:e + 1], courant_x, high[e:e + 1]], axis=0)
    cy = jnp.concatenate([low[e + 1:e + 2], courant_y, high[e + 1:e + 2]], axis=0)
    total = gram_rows(vectors, n)[1]
    inner, outer = (vectors, width - 4 * ny), (vectors, 4 * ny)
    acc = gram_scratch(vectors)
    cost = pl.CostEstimate(flops=12 * vectors * vectors * width, bytes_accessed=12 * vectors * width, transcendentals=0)
    v_inner, part = plain(interior_kernel, [inner, (total, T)], 2, [acc], cost=cost)(
        tangent.reshape(vectors * nx, ny), coefficients(courant_x, courant_y))
    v_outer, packed = plain(functools.partial(edge_kernel, nx), [outer, (total, T)], 5, [acc])(
        mine, low, high, coefficients(cx, cy), part)
    packed = all_reduce(packed, n)
    square = (vectors, vectors)
    row = (T, vectors)
    first_upper, q_inner, q_outer, packed = plain(
        functools.partial(first_kernel, cells), [square, inner, outer, (total, T)], 3, [square, row, square, acc], vectors,
    )(packed, v_inner, v_outer)
    packed = all_reduce(packed, n)
    basis, growth, log_growth = plain(
        functools.partial(second_kernel, cells), [(vectors * nx, ny), square, (vectors // T, T)], 4,
        [square, row, square, square], vectors,
    )(packed, q_inner, q_outer, first_upper)
    return basis.reshape(tangent.shape), growth, log_growth.reshape(vectors), first_upper


def solution(mesh):
    return jax.shard_map(
        body,
        mesh=mesh,
        in_specs=(P("runs", "space", None), P(("runs", "space"), None), P(("runs", "space"), None)),
        out_specs=(P("runs", "space", None), P("runs", None), P("runs"), P("runs", None)),
        check_vma=False,
    )
```

```python
import functools

import jax
import jax.numpy as jnp
from jax import lax
from jax.experimental import pallas as pl
from jax.experimental.pallas import tpu as pltpu
from jax.sharding import PartitionSpec as P

diffusion_number = 0.2
T = 128
B = 256
MICRO = 16
HIGHEST = lax.Precision.HIGHEST
MESH = pl.DeviceIdType.MESH
VMEM_LIMIT = 48 * 1024 * 1024


def dot(a, b, dims):
    return lax.dot_general(a, b, (dims, ((), ())), precision=HIGHEST, preferred_element_type=jnp.float32)


NN = ((1,), (0,))
NT = ((1,), (1,))
TN = ((0,), (0,))


def pair_list(blocks):
    return [(i, j) for i in range(blocks) for j in range(i, blocks)]


def gram_rows(vectors, devices):
    blocks = vectors // T
    rows = blocks * (blocks + 1) // 2 * T
    chunk = -(-rows // (devices * 8)) * 8
    return chunk, chunk * devices


def split(value):
    high = value.astype(jnp.bfloat16)
    rest = value - high.astype(jnp.float32)
    middle = rest.astype(jnp.bfloat16)
    low = (rest - middle.astype(jnp.float32)).astype(jnp.bfloat16)
    return high, middle, low


def parts_left(high, middle, low, axis):
    return jnp.concatenate([low, high, middle, middle, high, high], axis=axis)


def parts_right(high, middle, low, axis):
    return jnp.concatenate([high, low, middle, high, middle, high], axis=axis)


def product(a, b, dims):
    return lax.dot_general(a, b, (dims, ((), ())), preferred_element_type=jnp.float32)


def gram_into(v_refs, acc_ref):
    vectors = v_refs[0].shape[0]
    wide = vectors // B
    acc_ref[...] = jnp.zeros_like(acc_ref)
    for v_ref in v_refs:

        def step(s, _):
            cols = pl.ds(pl.multiple_of(s * B, B), B)
            parts = [split(v_ref[i * B:(i + 1) * B, cols]) for i in range(wide)]
            at = 0
            for i in range(wide):
                high, middle, low = parts[i]
                same = jnp.concatenate([middle, high], axis=1)
                acc_ref[at] += product(same, same, NT)
                mixed = jnp.concatenate([low, middle], axis=1)
                acc_ref[at + 1] += product(jnp.concatenate([high, high], axis=1), mixed, NT)
                at += 2
            for i in range(wide):
                for j in range(i + 1, wide):
                    acc_ref[at] += product(parts_left(*parts[i], 1), parts_right(*parts[j], 1), NT)
                    at += 1
            return 0

        lax.fori_loop(0, v_ref.shape[1] // B, step, 0)


def gram_scratch(vectors):
    wide = vectors // B
    return (2 * wide + wide * (wide - 1) // 2, B, B)


def pack(acc_ref, packed_ref, vectors, add_ref=None):
    wide = vectors // B
    blocks = {}
    for i in range(wide):
        mixed = acc_ref[2 * i + 1]
        blocks[i, i] = acc_ref[2 * i] + (mixed + mixed.T)
    at = 2 * wide
    for i in range(wide):
        for j in range(i + 1, wide):
            blocks[i, j] = acc_ref[at]
            at += 1
    r = B // T
    end = 0
    for i, j in pair_list(vectors // T):
        value = blocks[i // r, j // r][i % r * T:(i % r + 1) * T, j % r * T:(j % r + 1) * T]
        if add_ref is not None:
            value = value + add_ref[end:end + T, :]
        packed_ref[end:end + T, :] = value
        end += T
    if end < packed_ref.shape[0]:
        packed_ref[end:, :] = jnp.zeros((packed_ref.shape[0] - end, T), jnp.float32)


def lower_times(inverse_ref, split_refs, v_ref, emit):
    vectors, width = v_ref.shape
    wide = vectors // B

    def step(s, _):
        cols = pl.ds(pl.multiple_of(s * B, B), B)
        parts = [parts_right(*split(v_ref[k * B:(k + 1) * B, cols]), 0) for k in range(wide)]
        for i in range(wide):
            total = None
            for k in range(i + 1):
                left = parts_left(*[ref[i * B:(i + 1) * B, k * B:(k + 1) * B] for ref in split_refs], 1)
                term = product(left, parts[k], NN)
                total = term if total is None else total + term
            emit(i, s, cols, total)
        return 0

    lax.fori_loop(0, width // B, step, 0)


def split_into(inverse_ref, split_refs):
    for i in range(inverse_ref.shape[0] // T):
        here = slice(i * T, (i + 1) * T)
        for ref, value in zip(split_refs, split(inverse_ref[here, :])):
            ref[here, :] = value


def apply(west, center, east, coef_ref, e):
    ce, cw, cn, cs = [coef_ref[f, e:e + 1, :] for f in range(4)]
    north = pltpu.roll(center, T - 1, 1)
    south = pltpu.roll(center, 1, 1)
    return ((1.0 - 4.0 * diffusion_number) * center + (ce * east + cw * west)) + (cn * north + cs * south)


def two_steps(row, first, count, coef_ref, coef_at, store):
    zero = [row(first - 2), row(first - 1)]
    one = []
    for x in range(first - 1, first + count + 1):
        zero.append(row(x + 1))
        one.append(apply(*zero[-3:], coef_ref, coef_at(x)))
        if len(one) >= 3:
            store(x - 1, apply(*one[-3:], coef_ref, coef_at(x - 1)))


def interior_kernel(w_ref, coef_ref, v_ref, packed_ref, acc_ref):
    vectors = v_ref.shape[0]
    nx = v_ref.shape[1] // T + 4
    kc = 32

    def step(s, _):
        k0 = pl.multiple_of(s * kc, kc)

        def row(x):
            return w_ref[pl.ds(k0 * nx + x, kc, stride=nx), :]

        def store(x, value):
            v_ref[pl.ds(k0, kc), (x - 2) * T:(x - 1) * T] = value

        two_steps(row, 2, nx - 4, coef_ref, lambda x: x, store)
        return 0

    lax.fori_loop(0, vectors // kc, step, 0)
    gram_into([v_ref], acc_ref)
    pack(acc_ref, packed_ref, vectors)


def edge_kernel(nx, mine_ref, low_ref, high_ref, coef_ref, add_ref, v_ref, packed_ref, acc_ref):
    vectors = v_ref.shape[0]
    kc = 32

    def step(s, _):
        k0 = pl.multiple_of(s * kc, kc)

        def row(x):
            if x < 0:
                return low_ref[pl.ds((x + 2) * vectors + k0, kc), :]
            if x >= nx:
                return high_ref[pl.ds((x - nx) * vectors + k0, kc), :]
            at = x if x < 4 else x - nx + 8
            return mine_ref[pl.ds(at * vectors + k0, kc), :]

        def store(x, value):
            at = x if x < 2 else x - nx + 4
            v_ref[pl.ds(k0, kc), at * T:(at + 1) * T] = value

        two_steps(row, 0, 2, coef_ref, lambda x: x + 1, store)
        two_steps(row, nx - 2, 2, coef_ref, lambda x: x + 1, store)
        return 0

    lax.fori_loop(0, vectors // kc, step, 0)
    gram_into([v_ref], acc_ref)
    pack(acc_ref, packed_ref, vectors, add_ref)


def eliminate(block):
    m = MICRO
    lane = lax.broadcasted_iota(jnp.int32, (m, T), 1)
    sub = lax.broadcasted_iota(jnp.int32, (m, T), 0)
    rows128 = lax.broadcasted_iota(jnp.int32, (T, T), 0)
    lanes128 = lax.broadcasted_iota(jnp.int32, (T, T), 1)
    rest = jnp.concatenate([block, (rows128 == lanes128).astype(jnp.float32)], axis=1)
    uppers, inverses = [], []
    for p in range(T // m):
        panel = rest[:m]
        left = panel[:, :T]
        cols = [jnp.broadcast_to(left[:, p * m + j:p * m + j + 1], (m, T)) for j in range(m)]
        diag = jnp.ones((m, T), jnp.float32)
        for j in range(m):
            d = cols[j][j:j + 1, :]
            mult = jnp.where(sub > j, cols[j] * (1.0 / d), 0.0)
            diag = jnp.where(sub == j, d, diag)
            for k in range(j + 1, m):
                cols[k] = cols[k] - mult * cols[k][j:j + 1, :]
            wide = jnp.concatenate([mult, mult], axis=1)
            panel = panel - wide * panel[j:j + 1, :]
        scale = lax.rsqrt(diag)
        upper = jnp.where(lane >= sub + p * m, panel[:, :T] * scale, 0.0)
        inverse = panel[:, T:] * scale
        uppers.append(upper)
        inverses.append(inverse)
        if p + 1 < T // m:
            both = split(jnp.concatenate([upper, inverse], axis=1))
            left = parts_left(*[part[:, :T] for part in both], 0)
            rest = rest[m:] - product(left, parts_right(*both, 0), TN)[(p + 1) * m:]
    return jnp.concatenate(uppers, axis=0), jnp.concatenate(inverses, axis=0)


def factor_into(packed_ref, cells, z_ref, row_ref, upper_ref, inverse_ref, left_ref, right_ref):
    vectors = z_ref.shape[0]
    blocks = vectors // T
    z_ref[...] = jnp.zeros_like(z_ref)
    for at, (i, j) in enumerate(pair_list(blocks)):
        z_ref[i * T:(i + 1) * T, j * T:(j + 1) * T] = packed_ref[at * T:(at + 1) * T, :] / cells
    block_of = lax.broadcasted_iota(jnp.int32, (T, vectors), 1) // T

    def step(b, _):
        here = pl.ds(pl.multiple_of(b * T, T), T)
        upper, inverse = eliminate(z_ref[here, here])
        row_ref[...] = product(parts_left(*split(inverse), 1), parts_right(*split(z_ref[here, :]), 0), NN)
        row_ref[:, here] = inverse
        row = row_ref[...]
        parts = split(row)
        left_ref[...] = parts_left(*parts, 0)
        right_ref[...] = parts_right(*parts, 0)
        upper_ref[here, :] = jnp.where(block_of > b, row, 0.0)
        upper_ref[here, here] = upper
        inverse_ref[here, :] = jnp.where(block_of <= b, row, 0.0)

        def below(c, _):
            there = pl.ds(pl.multiple_of(c * T, T), T)
            old = jnp.where(block_of == b, 0.0, z_ref[there, :])
            z_ref[there, :] = old - product(left_ref[:, there], right_ref[...], TN)
            return 0

        lax.fori_loop(b + 1, blocks, below, 0)
        return 0

    lax.fori_loop(0, blocks, step, 0)


def first_kernel(cells, packed_ref, inner_ref, outer_ref, upper_ref, q_inner_ref, q_outer_ref, out_ref, z_ref, row_ref, inverse_ref, acc_ref, left_ref, right_ref, *split_refs):
    vectors = inner_ref.shape[0]
    factor_into(packed_ref, cells, z_ref, row_ref, upper_ref, inverse_ref, left_ref, right_ref)
    split_into(inverse_ref, split_refs)
    for v_ref, q_ref in ((inner_ref, q_inner_ref), (outer_ref, q_outer_ref)):

        def emit(i, s, cols, value):
            q_ref[i * B:(i + 1) * B, cols] = value

        lower_times(inverse_ref, split_refs, v_ref, emit)
    gram_into([q_inner_ref, q_outer_ref], acc_ref)
    pack(acc_ref, out_ref, vectors)


def second_kernel(cells, packed_ref, inner_ref, outer_ref, first_ref, basis_ref, growth_ref, log_ref, z_ref, row_ref, inverse_ref, upper_ref, left_ref, right_ref, *split_refs):
    vectors = inner_ref.shape[0]
    nx = basis_ref.shape[0] // vectors
    factor_into(packed_ref, cells, z_ref, row_ref, upper_ref, inverse_ref, left_ref, right_ref)
    split_into(inverse_ref, split_refs)

    def emit_inner(i, s, cols, value):
        for h in range(2):
            basis_ref[pl.ds(i * B * nx + 2 + 2 * s + h, B, stride=nx), :] = value[:, h * T:(h + 1) * T]

    def emit_outer(i, s, cols, value):
        for h in range(2):
            basis_ref[pl.ds(i * B * nx + s * (nx - 2) + h, B, stride=nx), :] = value[:, h * T:(h + 1) * T]

    lower_times(inverse_ref, split_refs, inner_ref, emit_inner)
    lower_times(inverse_ref, split_refs, outer_ref, emit_outer)
    rows = lax.broadcasted_iota(jnp.int32, (T, T), 0)
    lanes = lax.broadcasted_iota(jnp.int32, (T, T), 1)
    for i in range(vectors // T):
        here = slice(i * T, (i + 1) * T)
        growth_ref[here, :] = dot(upper_ref[here, i * T:], first_ref[i * T:, :], NN)
        one = jnp.sum(jnp.where(rows == lanes, first_ref[here, here], 0.0), axis=0, keepdims=True)
        two = jnp.sum(jnp.where(rows == lanes, upper_ref[here, here], 0.0), axis=0, keepdims=True)
        log_ref[i:i + 1, :] = jnp.log(one) + jnp.log(two)


def reduce_kernel(n, x_ref, o_ref, swap_buf, y_out, y_in, z_out, z_in, sw_s, sw_r, y_s, y_r, z_s, z_r, zg_s, zg_r, yg_s, yg_r, cf_s, cf_r):
    groups = n // 4
    chunk = x_ref.shape[0] // n
    me = lax.axis_index("space")
    core = me % 2
    side = (me // 2) % 2
    group = me // 4
    core_peer = group * 4 + side * 2 + (1 - core)
    side_peer = group * 4 + (1 - side) * 2 + core

    def to(k):
        return lax.rem(group + k, groups)

    def source(k):
        return lax.rem(group + groups - k, groups)

    def rows(c, y, g):
        return pl.ds(pl.multiple_of(((c * 2 + y) * groups + g) * chunk, 8), chunk)

    def y_of(q):
        return q * side + (1 - q) * (1 - side)

    def copy(src, dst, send, recv, device):
        return pltpu.make_async_remote_copy(
            src_ref=src, dst_ref=dst, send_sem=send, recv_sem=recv,
            device_id={"space": device}, device_id_type=MESH)

    def z_peer(k):
        return to(k) * 4 + side * 2 + core

    def swap(q, k):
        at = q * groups + k
        return copy(x_ref.at[rows(1 - core, y_of(q), to(k))], swap_buf.at[at], sw_s.at[at], sw_r.at[at], core_peer)

    def across(k):
        return copy(y_out.at[k], y_in.at[k], y_s.at[k], y_r.at[k], side_peer)

    def scatter(k):
        return copy(z_out.at[k], z_in.at[k], z_s.at[k], z_r.at[k], z_peer(k))

    def gather(k):
        own = o_ref.at[rows(core, side, group)]
        return copy(own, own, zg_s.at[k], zg_r.at[k], z_peer(k))

    def side_forward(k):
        at = o_ref.at[rows(core, side, source(k))]
        return copy(at, at, yg_s.at[k], yg_r.at[k], side_peer)

    def core_forward(q, k):
        at = o_ref.at[rows(core, y_of(q), source(k))]
        sem = q * groups + k
        return copy(at, at, cf_s.at[sem], cf_r.at[sem], core_peer)

    def loop(low, high, call):
        def step(k, _):
            call(k)
            return 0

        lax.fori_loop(low, high, step, 0)

    barrier = pltpu.get_barrier_semaphore()

    def greet(device):
        pl.semaphore_signal(barrier, inc=1, device_id={"space": device}, device_id_type=MESH)

    greet(core_peer)
    greet(side_peer)
    loop(1, groups, lambda k: greet(z_peer(k)))
    pl.semaphore_wait(barrier, groups + 1)

    for q in range(2):
        loop(1, groups + 1, lambda k: swap(q, lax.rem(k, groups)).start())

    def send_across(i):
        k = lax.rem(i, groups)
        swap(0, k).wait_recv()
        y_out[k] = x_ref[rows(core, 1 - side, to(k)), :] + swap_buf[k]
        across(k).start()

    loop(1, groups + 1, send_across)

    def combined(k):
        swap(1, k).wait_recv()
        across(k).wait_recv()
        return x_ref[rows(core, side, to(k)), :] + swap_buf[groups + k] + y_in[k]

    def send_out(k):
        z_out[k] = combined(k)
        scatter(k).start()

    loop(1, groups, send_out)

    def add(k, acc):
        scatter(k).wait_recv()
        return acc + z_in[k]

    o_ref[rows(core, side, group), :] = lax.fori_loop(1, groups, add, combined(0))

    loop(1, groups, lambda k: gather(k).start())
    side_forward(0).start()
    core_forward(1, 0).start()

    def pass_z(k):
        gather(k).wait_recv()
        side_forward(k).start()
        core_forward(1, k).start()

    loop(1, groups, pass_z)

    def arrived(k):
        there = o_ref.at[rows(core, 1 - side, source(k))]
        return copy(there, there, yg_s.at[k], yg_r.at[k], side_peer)

    def pass_side(k):
        arrived(k).wait_recv()
        core_forward(0, k).start()

    loop(0, groups, pass_side)

    def finish(k):
        for q in range(2):
            there = o_ref.at[rows(1 - core, y_of(q), source(k))]
            sem = q * groups + k
            copy(there, there, cf_s.at[sem], cf_r.at[sem], core_peer).wait_recv()
            core_forward(q, k).wait_send()
            swap(q, k).wait_send()
        across(k).wait_send()
        side_forward(k).wait_send()

    loop(0, groups, finish)

    def drain(k):
        scatter(k).wait_send()
        gather(k).wait_send()

    loop(1, groups, drain)


def whole(memory=pltpu.VMEM):
    return pl.BlockSpec(memory_space=memory)


def plain(kernel, outs, ins, scratch=(), splits=0, cost=None):
    scratch_shapes = [pltpu.VMEM(shape, jnp.float32) for shape in scratch]
    if splits:
        scratch_shapes += [pltpu.VMEM((6 * T, splits), jnp.bfloat16)] * 2 + [pltpu.VMEM((splits, splits), jnp.bfloat16)] * 3
    return pl.pallas_call(
        kernel,
        out_shape=tuple(jax.ShapeDtypeStruct(shape, jnp.float32) for shape in outs),
        in_specs=[whole()] * ins,
        out_specs=tuple(whole() for _ in outs),
        scratch_shapes=scratch_shapes,
        compiler_params=pltpu.CompilerParams(vmem_limit_bytes=VMEM_LIMIT),
        cost_estimate=cost,
    )


def all_reduce(packed, n):
    groups = n // 4
    chunk = packed.shape[0] // n
    sems = pltpu.SemaphoreType.DMA
    pairs = [sems((2 * groups,))] * 2
    singles = [sems((groups,))] * 2
    return pl.pallas_call(
        functools.partial(reduce_kernel, n),
        out_shape=jax.ShapeDtypeStruct(packed.shape, jnp.float32),
        in_specs=[whole()],
        out_specs=whole(),
        scratch_shapes=[pltpu.VMEM((2 * groups, chunk, T), jnp.float32)]
        + [pltpu.VMEM((groups, chunk, T), jnp.float32)] * 4
        + pairs + singles * 4 + pairs,
        compiler_params=pltpu.CompilerParams(collective_id=0, has_side_effects=True, vmem_limit_bytes=VMEM_LIMIT),
    )(packed)


def body(tangent, courant_x, courant_y):
    vectors, nx, ny = tangent.shape
    n = lax.axis_size("space")
    width = nx * ny
    cells = float(width * n)

    pick = jnp.concatenate([tangent[:, :4], tangent[:, nx - 4:]], axis=1)
    mine = jnp.transpose(pick, (1, 0, 2)).reshape(8 * vectors, ny)

    def edge(a, b):
        rows = mine[a * vectors:(a + 2) * vectors]
        return jnp.concatenate([rows, courant_x[b:b + 1], courant_y[b:b + 1], jnp.zeros((6, ny), jnp.float32)], axis=0)

    def coefficients(x, y):
        x, y = 0.5 * x, 0.5 * y
        return jnp.stack([diffusion_number - x, diffusion_number + x, diffusion_number - y, diffusion_number + y])

    low = lax.ppermute(edge(6, nx - 1), "space", [(i, (i + 1) % n) for i in range(n)])
    high = lax.ppermute(edge(0, 0), "space", [((i + 1) % n, i) for i in range(n)])
    e = 2 * vectors
    cx = jnp.concatenate([low[e:e + 1], courant_x, high[e:e + 1]], axis=0)
    cy = jnp.concatenate([low[e + 1:e + 2], courant_y, high[e + 1:e + 2]], axis=0)
    total = gram_rows(vectors, n)[1]
    inner, outer = (vectors, width - 4 * ny), (vectors, 4 * ny)
    acc = gram_scratch(vectors)
    cost = pl.CostEstimate(flops=12 * vectors * vectors * width, bytes_accessed=12 * vectors * width, transcendentals=0)
    v_inner, part = plain(interior_kernel, [inner, (total, T)], 2, [acc], cost=cost)(
        tangent.reshape(vectors * nx, ny), coefficients(courant_x, courant_y))
    v_outer, packed = plain(functools.partial(edge_kernel, nx), [outer, (total, T)], 5, [acc])(
        mine, low, high, coefficients(cx, cy), part)
    packed = all_reduce(packed, n)
    square = (vectors, vectors)
    row = (T, vectors)
    first_upper, q_inner, q_outer, packed = plain(
        functools.partial(first_kernel, cells), [square, inner, outer, (total, T)], 3, [square, row, square, acc], vectors,
    )(packed, v_inner, v_outer)
    packed = all_reduce(packed, n)
    basis, growth, log_growth = plain(
        functools.partial(second_kernel, cells), [(vectors * nx, ny), square, (vectors // T, T)], 4,
        [square, row, square, square], vectors,
    )(packed, q_inner, q_outer, first_upper)
    return basis.reshape(tangent.shape), growth, log_growth.reshape(vectors), first_upper


def solution(mesh):
    return jax.shard_map(
        body,
        mesh=mesh,
        in_specs=(P("runs", "space", None), P(("runs", "space"), None), P(("runs", "space"), None)),
        out_specs=(P("runs", "space", None), P("runs", None), P("runs"), P("runs", None)),
        check_vma=False,
    )
```

```python
import functools

import jax
import jax.numpy as jnp
from jax import lax
from jax.experimental import pallas as pl
from jax.experimental.pallas import tpu as pltpu
from jax.sharding import PartitionSpec as P

diffusion_number = 0.2
T = 128
B = 256
MICRO = 16
HIGHEST = lax.Precision.HIGHEST
MESH = pl.DeviceIdType.MESH
VMEM_LIMIT = 48 * 1024 * 1024


def dot(a, b, dims):
    return lax.dot_general(a, b, (dims, ((), ())), precision=HIGHEST, preferred_element_type=jnp.float32)


NN = ((1,), (0,))
NT = ((1,), (1,))
TN = ((0,), (0,))


def pair_list(blocks):
    return [(i, j) for i in range(blocks) for j in range(i, blocks)]


def gram_rows(vectors, devices):
    blocks = vectors // T
    rows = blocks * (blocks + 1) // 2 * T
    chunk = -(-rows // (devices * 8)) * 8
    return chunk, chunk * devices


def split(value):
    high = value.astype(jnp.bfloat16)
    rest = value - high.astype(jnp.float32)
    middle = rest.astype(jnp.bfloat16)
    low = (rest - middle.astype(jnp.float32)).astype(jnp.bfloat16)
    return high, middle, low


def parts_left(high, middle, low, axis):
    return jnp.concatenate([low, high, middle, middle, high, high], axis=axis)


def parts_right(high, middle, low, axis):
    return jnp.concatenate([high, low, middle, high, middle, high], axis=axis)


def product(a, b, dims):
    return lax.dot_general(a, b, (dims, ((), ())), preferred_element_type=jnp.float32)


def gram_into(v_refs, acc_ref):
    vectors = v_refs[0].shape[0]
    wide = vectors // B
    acc_ref[...] = jnp.zeros_like(acc_ref)
    for v_ref in v_refs:

        def step(s, _):
            cols = pl.ds(pl.multiple_of(s * B, B), B)
            parts = [split(v_ref[i * B:(i + 1) * B, cols]) for i in range(wide)]
            at = 0
            for i in range(wide):
                high, middle, low = parts[i]
                same = jnp.concatenate([middle, high], axis=1)
                acc_ref[at] += product(same, same, NT)
                mixed = jnp.concatenate([low, middle], axis=1)
                acc_ref[at + 1] += product(jnp.concatenate([high, high], axis=1), mixed, NT)
                at += 2
            for i in range(wide):
                for j in range(i + 1, wide):
                    acc_ref[at] += product(parts_left(*parts[i], 1), parts_right(*parts[j], 1), NT)
                    at += 1
            return 0

        lax.fori_loop(0, v_ref.shape[1] // B, step, 0)


def gram_scratch(vectors):
    wide = vectors // B
    return (2 * wide + wide * (wide - 1) // 2, B, B)


def pack(acc_ref, packed_ref, vectors, add_ref=None):
    wide = vectors // B
    blocks = {}
    for i in range(wide):
        mixed = acc_ref[2 * i + 1]
        blocks[i, i] = acc_ref[2 * i] + (mixed + mixed.T)
    at = 2 * wide
    for i in range(wide):
        for j in range(i + 1, wide):
            blocks[i, j] = acc_ref[at]
            at += 1
    r = B // T
    end = 0
    for i, j in pair_list(vectors // T):
        value = blocks[i // r, j // r][i % r * T:(i % r + 1) * T, j % r * T:(j % r + 1) * T]
        if add_ref is not None:
            value = value + add_ref[end:end + T, :]
        packed_ref[end:end + T, :] = value
        end += T
    if end < packed_ref.shape[0]:
        packed_ref[end:, :] = jnp.zeros((packed_ref.shape[0] - end, T), jnp.float32)


def lower_times(inverse_ref, split_refs, v_ref, emit):
    vectors, width = v_ref.shape
    wide = vectors // B

    def step(s, _):
        cols = pl.ds(pl.multiple_of(s * B, B), B)
        parts = [parts_right(*split(v_ref[k * B:(k + 1) * B, cols]), 0) for k in range(wide)]
        for i in range(wide):
            total = None
            for k in range(i + 1):
                left = parts_left(*[ref[i * B:(i + 1) * B, k * B:(k + 1) * B] for ref in split_refs], 1)
                term = product(left, parts[k], NN)
                total = term if total is None else total + term
            emit(i, s, cols, total)
        return 0

    lax.fori_loop(0, width // B, step, 0)


def split_into(inverse_ref, split_refs):
    for i in range(inverse_ref.shape[0] // T):
        here = slice(i * T, (i + 1) * T)
        for ref, value in zip(split_refs, split(inverse_ref[here, :])):
            ref[here, :] = value


def apply(west, center, east, coef_ref, e):
    ce, cw, cn, cs = [coef_ref[f, e:e + 1, :] for f in range(4)]
    north = pltpu.roll(center, T - 1, 1)
    south = pltpu.roll(center, 1, 1)
    return ((1.0 - 4.0 * diffusion_number) * center + (ce * east + cw * west)) + (cn * north + cs * south)


def two_steps(row, first, count, coef_ref, coef_at, store):
    zero = [row(first - 2), row(first - 1)]
    one = []
    for x in range(first - 1, first + count + 1):
        zero.append(row(x + 1))
        one.append(apply(*zero[-3:], coef_ref, coef_at(x)))
        if len(one) >= 3:
            store(x - 1, apply(*one[-3:], coef_ref, coef_at(x - 1)))


def pick_kernel(w_ref, cx_ref, cy_ref, mine_ref, low_ref, high_ref):
    nx = cx_ref.shape[0]
    vectors = w_ref.shape[0] // nx
    for at in range(8):
        x = at if at < 4 else nx - 8 + at
        value = w_ref[pl.ds(x, vectors, stride=nx), :]
        mine_ref[at * vectors:(at + 1) * vectors, :] = value
        if at < 2:
            high_ref[at * vectors:(at + 1) * vectors, :] = value
        if at >= 6:
            low_ref[(at - 6) * vectors:(at - 5) * vectors, :] = value
    zeros = jnp.zeros((6, T), jnp.float32)
    for ref, x in ((low_ref, nx - 1), (high_ref, 0)):
        ref[2 * vectors:, :] = jnp.concatenate([cx_ref[x:x + 1, :], cy_ref[x:x + 1, :], zeros], axis=0)


def interior_kernel(w_ref, coef_ref, v_ref, packed_ref, acc_ref):
    vectors = v_ref.shape[0]
    nx = v_ref.shape[1] // T + 4
    kc = 32

    def step(s, _):
        k0 = pl.multiple_of(s * kc, kc)

        def row(x):
            return w_ref[pl.ds(k0 * nx + x, kc, stride=nx), :]

        def store(x, value):
            v_ref[pl.ds(k0, kc), (x - 2) * T:(x - 1) * T] = value

        two_steps(row, 2, nx - 4, coef_ref, lambda x: x, store)
        return 0

    lax.fori_loop(0, vectors // kc, step, 0)
    gram_into([v_ref], acc_ref)
    pack(acc_ref, packed_ref, vectors)


def edge_kernel(nx, mine_ref, low_ref, high_ref, coef_ref, add_ref, v_ref, packed_ref, acc_ref):
    vectors = v_ref.shape[0]
    kc = 32

    def step(s, _):
        k0 = pl.multiple_of(s * kc, kc)

        def row(x):
            if x < 0:
                return low_ref[pl.ds((x + 2) * vectors + k0, kc), :]
            if x >= nx:
                return high_ref[pl.ds((x - nx) * vectors + k0, kc), :]
            at = x if x < 4 else x - nx + 8
            return mine_ref[pl.ds(at * vectors + k0, kc), :]

        def store(x, value):
            at = x if x < 2 else x - nx + 4
            v_ref[pl.ds(k0, kc), at * T:(at + 1) * T] = value

        two_steps(row, 0, 2, coef_ref, lambda x: x + 1, store)
        two_steps(row, nx - 2, 2, coef_ref, lambda x: x + 1, store)
        return 0

    lax.fori_loop(0, vectors // kc, step, 0)
    gram_into([v_ref], acc_ref)
    pack(acc_ref, packed_ref, vectors, add_ref)


def eliminate(block):
    m = MICRO
    lane = lax.broadcasted_iota(jnp.int32, (m, T), 1)
    sub = lax.broadcasted_iota(jnp.int32, (m, T), 0)
    rows128 = lax.broadcasted_iota(jnp.int32, (T, T), 0)
    lanes128 = lax.broadcasted_iota(jnp.int32, (T, T), 1)
    rest = jnp.concatenate([block, (rows128 == lanes128).astype(jnp.float32)], axis=1)
    uppers, inverses = [], []
    for p in range(T // m):
        panel = rest[:m]
        left = panel[:, :T]
        cols = [jnp.broadcast_to(left[:, p * m + j:p * m + j + 1], (m, T)) for j in range(m)]
        diag = jnp.ones((m, T), jnp.float32)
        for j in range(m):
            d = cols[j][j:j + 1, :]
            mult = jnp.where(sub > j, cols[j] * (1.0 / d), 0.0)
            diag = jnp.where(sub == j, d, diag)
            for k in range(j + 1, m):
                cols[k] = cols[k] - mult * cols[k][j:j + 1, :]
            wide = jnp.concatenate([mult, mult], axis=1)
            panel = panel - wide * panel[j:j + 1, :]
        scale = lax.rsqrt(diag)
        upper = jnp.where(lane >= sub + p * m, panel[:, :T] * scale, 0.0)
        inverse = panel[:, T:] * scale
        uppers.append(upper)
        inverses.append(inverse)
        if p + 1 < T // m:
            both = split(jnp.concatenate([upper, inverse], axis=1))
            left = parts_left(*[part[:, :T] for part in both], 0)
            rest = rest[m:] - product(left, parts_right(*both, 0), TN)[(p + 1) * m:]
    return jnp.concatenate(uppers, axis=0), jnp.concatenate(inverses, axis=0)


def factor_into(packed_ref, cells, z_ref, row_ref, upper_ref, inverse_ref, left_ref, right_ref):
    vectors = z_ref.shape[0]
    blocks = vectors // T
    z_ref[...] = jnp.zeros_like(z_ref)
    for at, (i, j) in enumerate(pair_list(blocks)):
        z_ref[i * T:(i + 1) * T, j * T:(j + 1) * T] = packed_ref[at * T:(at + 1) * T, :] / cells
    block_of = lax.broadcasted_iota(jnp.int32, (T, vectors), 1) // T

    def step(b, _):
        here = pl.ds(pl.multiple_of(b * T, T), T)
        upper, inverse = eliminate(z_ref[here, here])
        row_ref[...] = product(parts_left(*split(inverse), 1), parts_right(*split(z_ref[here, :]), 0), NN)
        row_ref[:, here] = inverse
        row = row_ref[...]
        parts = split(row)
        left_ref[...] = parts_left(*parts, 0)
        right_ref[...] = parts_right(*parts, 0)
        upper_ref[here, :] = jnp.where(block_of > b, row, 0.0)
        upper_ref[here, here] = upper
        inverse_ref[here, :] = jnp.where(block_of <= b, row, 0.0)

        def below(c, _):
            there = pl.ds(pl.multiple_of(c * T, T), T)
            old = jnp.where(block_of == b, 0.0, z_ref[there, :])
            z_ref[there, :] = old - product(left_ref[:, there], right_ref[...], TN)
            return 0

        lax.fori_loop(b + 1, blocks, below, 0)
        return 0

    lax.fori_loop(0, blocks, step, 0)


def first_kernel(cells, packed_ref, inner_ref, outer_ref, upper_ref, q_inner_ref, q_outer_ref, out_ref, z_ref, row_ref, inverse_ref, acc_ref, left_ref, right_ref, *split_refs):
    vectors = inner_ref.shape[0]
    factor_into(packed_ref, cells, z_ref, row_ref, upper_ref, inverse_ref, left_ref, right_ref)
    split_into(inverse_ref, split_refs)
    for v_ref, q_ref in ((inner_ref, q_inner_ref), (outer_ref, q_outer_ref)):

        def emit(i, s, cols, value):
            q_ref[i * B:(i + 1) * B, cols] = value

        lower_times(inverse_ref, split_refs, v_ref, emit)
    gram_into([q_inner_ref, q_outer_ref], acc_ref)
    pack(acc_ref, out_ref, vectors)


def second_kernel(cells, packed_ref, inner_ref, outer_ref, first_ref, basis_ref, growth_ref, log_ref, z_ref, row_ref, inverse_ref, upper_ref, left_ref, right_ref, *split_refs):
    vectors = inner_ref.shape[0]
    nx = basis_ref.shape[0] // vectors
    factor_into(packed_ref, cells, z_ref, row_ref, upper_ref, inverse_ref, left_ref, right_ref)
    split_into(inverse_ref, split_refs)

    def emit_inner(i, s, cols, value):
        for h in range(2):
            basis_ref[pl.ds(i * B * nx + 2 + 2 * s + h, B, stride=nx), :] = value[:, h * T:(h + 1) * T]

    def emit_outer(i, s, cols, value):
        for h in range(2):
            basis_ref[pl.ds(i * B * nx + s * (nx - 2) + h, B, stride=nx), :] = value[:, h * T:(h + 1) * T]

    lower_times(inverse_ref, split_refs, inner_ref, emit_inner)
    lower_times(inverse_ref, split_refs, outer_ref, emit_outer)
    rows = lax.broadcasted_iota(jnp.int32, (T, T), 0)
    lanes = lax.broadcasted_iota(jnp.int32, (T, T), 1)
    for i in range(vectors // T):
        here = slice(i * T, (i + 1) * T)
        growth_ref[here, :] = dot(upper_ref[here, i * T:], first_ref[i * T:, :], NN)
        one = jnp.sum(jnp.where(rows == lanes, first_ref[here, here], 0.0), axis=0, keepdims=True)
        two = jnp.sum(jnp.where(rows == lanes, upper_ref[here, here], 0.0), axis=0, keepdims=True)
        log_ref[i:i + 1, :] = jnp.log(one) + jnp.log(two)


def reduce_kernel(n, x_ref, o_ref, swap_buf, y_out, y_in, z_out, z_in, sw_s, sw_r, y_s, y_r, z_s, z_r, zg_s, zg_r, yg_s, yg_r, cf_s, cf_r):
    groups = n // 4
    chunk = x_ref.shape[0] // n
    me = lax.axis_index("space")
    core = me % 2
    side = (me // 2) % 2
    group = me // 4
    core_peer = group * 4 + side * 2 + (1 - core)
    side_peer = group * 4 + (1 - side) * 2 + core

    def to(k):
        return lax.rem(group + k, groups)

    def source(k):
        return lax.rem(group + groups - k, groups)

    def rows(c, y, g):
        return pl.ds(pl.multiple_of(((c * 2 + y) * groups + g) * chunk, 8), chunk)

    def y_of(q):
        return q * side + (1 - q) * (1 - side)

    def copy(src, dst, send, recv, device):
        return pltpu.make_async_remote_copy(
            src_ref=src, dst_ref=dst, send_sem=send, recv_sem=recv,
            device_id={"space": device}, device_id_type=MESH)

    def z_peer(k):
        return to(k) * 4 + side * 2 + core

    def swap(q, k):
        at = q * groups + k
        return copy(x_ref.at[rows(1 - core, y_of(q), to(k))], swap_buf.at[at], sw_s.at[at], sw_r.at[at], core_peer)

    def across(k):
        return copy(y_out.at[k], y_in.at[k], y_s.at[k], y_r.at[k], side_peer)

    def scatter(k):
        return copy(z_out.at[k], z_in.at[k], z_s.at[k], z_r.at[k], z_peer(k))

    def gather(k):
        own = o_ref.at[rows(core, side, group)]
        return copy(own, own, zg_s.at[k], zg_r.at[k], z_peer(k))

    def side_forward(k):
        at = o_ref.at[rows(core, side, source(k))]
        return copy(at, at, yg_s.at[k], yg_r.at[k], side_peer)

    def core_forward(q, k):
        at = o_ref.at[rows(core, y_of(q), source(k))]
        sem = q * groups + k
        return copy(at, at, cf_s.at[sem], cf_r.at[sem], core_peer)

    def loop(low, high, call):
        def step(k, _):
            call(k)
            return 0

        lax.fori_loop(low, high, step, 0)

    barrier = pltpu.get_barrier_semaphore()

    def greet(device):
        pl.semaphore_signal(barrier, inc=1, device_id={"space": device}, device_id_type=MESH)

    greet(core_peer)
    greet(side_peer)
    loop(1, groups, lambda k: greet(z_peer(k)))
    pl.semaphore_wait(barrier, groups + 1)

    for q in range(2):
        loop(1, groups + 1, lambda k: swap(q, lax.rem(k, groups)).start())

    def send_across(i):
        k = lax.rem(i, groups)
        swap(0, k).wait_recv()
        y_out[k] = x_ref[rows(core, 1 - side, to(k)), :] + swap_buf[k]
        across(k).start()

    loop(1, groups + 1, send_across)

    def combined(k):
        swap(1, k).wait_recv()
        across(k).wait_recv()
        return x_ref[rows(core, side, to(k)), :] + swap_buf[groups + k] + y_in[k]

    def send_out(k):
        z_out[k] = combined(k)
        scatter(k).start()

    loop(1, groups, send_out)

    def add(k, acc):
        scatter(k).wait_recv()
        return acc + z_in[k]

    o_ref[rows(core, side, group), :] = lax.fori_loop(1, groups, add, combined(0))

    loop(1, groups, lambda k: gather(k).start())
    side_forward(0).start()
    core_forward(1, 0).start()

    def pass_z(k):
        gather(k).wait_recv()
        side_forward(k).start()
        core_forward(1, k).start()

    loop(1, groups, pass_z)

    def arrived(k):
        there = o_ref.at[rows(core, 1 - side, source(k))]
        return copy(there, there, yg_s.at[k], yg_r.at[k], side_peer)

    def pass_side(k):
        arrived(k).wait_recv()
        core_forward(0, k).start()

    loop(0, groups, pass_side)

    def finish(k):
        for q in range(2):
            there = o_ref.at[rows(1 - core, y_of(q), source(k))]
            sem = q * groups + k
            copy(there, there, cf_s.at[sem], cf_r.at[sem], core_peer).wait_recv()
            core_forward(q, k).wait_send()
            swap(q, k).wait_send()
        across(k).wait_send()
        side_forward(k).wait_send()

    loop(0, groups, finish)

    def drain(k):
        scatter(k).wait_send()
        gather(k).wait_send()

    loop(1, groups, drain)


def whole(memory=pltpu.VMEM):
    return pl.BlockSpec(memory_space=memory)


def plain(kernel, outs, ins, scratch=(), splits=0, cost=None):
    scratch_shapes = [pltpu.VMEM(shape, jnp.float32) for shape in scratch]
    if splits:
        scratch_shapes += [pltpu.VMEM((6 * T, splits), jnp.bfloat16)] * 2 + [pltpu.VMEM((splits, splits), jnp.bfloat16)] * 3
    return pl.pallas_call(
        kernel,
        out_shape=tuple(jax.ShapeDtypeStruct(shape, jnp.float32) for shape in outs),
        in_specs=[whole()] * ins,
        out_specs=tuple(whole() for _ in outs),
        scratch_shapes=scratch_shapes,
        compiler_params=pltpu.CompilerParams(vmem_limit_bytes=VMEM_LIMIT),
        cost_estimate=cost,
    )


def all_reduce(packed, n):
    groups = n // 4
    chunk = packed.shape[0] // n
    sems = pltpu.SemaphoreType.DMA
    pairs = [sems((2 * groups,))] * 2
    singles = [sems((groups,))] * 2
    return pl.pallas_call(
        functools.partial(reduce_kernel, n),
        out_shape=jax.ShapeDtypeStruct(packed.shape, jnp.float32),
        in_specs=[whole()],
        out_specs=whole(),
        scratch_shapes=[pltpu.VMEM((2 * groups, chunk, T), jnp.float32)]
        + [pltpu.VMEM((groups, chunk, T), jnp.float32)] * 4
        + pairs + singles * 4 + pairs,
        compiler_params=pltpu.CompilerParams(collective_id=0, has_side_effects=True, vmem_limit_bytes=VMEM_LIMIT),
    )(packed)


def body(tangent, courant_x, courant_y):
    vectors, nx, ny = tangent.shape
    n = lax.axis_size("space")
    width = nx * ny
    cells = float(width * n)

    flat = tangent.reshape(vectors * nx, ny)
    sent = (2 * vectors + 8, ny)
    mine, low, high = plain(pick_kernel, [(8 * vectors, ny), sent, sent], 3)(flat, courant_x, courant_y)

    def coefficients(x, y):
        x, y = 0.5 * x, 0.5 * y
        return jnp.stack([diffusion_number - x, diffusion_number + x, diffusion_number - y, diffusion_number + y])

    low = lax.ppermute(low, "space", [(i, (i + 1) % n) for i in range(n)])
    high = lax.ppermute(high, "space", [((i + 1) % n, i) for i in range(n)])
    e = 2 * vectors
    cx = jnp.concatenate([low[e:e + 1], courant_x, high[e:e + 1]], axis=0)
    cy = jnp.concatenate([low[e + 1:e + 2], courant_y, high[e + 1:e + 2]], axis=0)
    total = gram_rows(vectors, n)[1]
    inner, outer = (vectors, width - 4 * ny), (vectors, 4 * ny)
    acc = gram_scratch(vectors)
    cost = pl.CostEstimate(flops=12 * vectors * vectors * width, bytes_accessed=12 * vectors * width, transcendentals=0)
    v_inner, part = plain(interior_kernel, [inner, (total, T)], 2, [acc], cost=cost)(
        flat, coefficients(courant_x, courant_y))
    v_outer, packed = plain(functools.partial(edge_kernel, nx), [outer, (total, T)], 5, [acc])(
        mine, low, high, coefficients(cx, cy), part)
    packed = all_reduce(packed, n)
    square = (vectors, vectors)
    row = (T, vectors)
    first_upper, q_inner, q_outer, packed = plain(
        functools.partial(first_kernel, cells), [square, inner, outer, (total, T)], 3, [square, row, square, acc], vectors,
    )(packed, v_inner, v_outer)
    packed = all_reduce(packed, n)
    basis, growth, log_growth = plain(
        functools.partial(second_kernel, cells), [(vectors * nx, ny), square, (vectors // T, T)], 4,
        [square, row, square, square], vectors,
    )(packed, q_inner, q_outer, first_upper)
    return basis.reshape(tangent.shape), growth, log_growth.reshape(vectors), first_upper


def solution(mesh):
    return jax.shard_map(
        body,
        mesh=mesh,
        in_specs=(P("runs", "space", None), P(("runs", "space"), None), P(("runs", "space"), None)),
        out_specs=(P("runs", "space", None), P("runs", None), P("runs"), P("runs", None)),
        check_vma=False,
    )
```
